32 devices in a mesh: section: 4 (over z), expert: 8 (over y, x, core).
Axes of the slice: x: 2, y: 2, z: 4, core: 2. Of those that a mesh axis runs over, the one named last changes fastest.
Arguments:
- tokens_in: bfloat16 [4, 128, 4096], P('section', 'expert'), may hold values from -6 to 6
- out_grad: bfloat16 [4, 128, 4096], P('section', 'expert'), may hold values from -6 to 6
- expert_ids: int32 [4, 128, 2], P('section', 'expert'), may hold values from 0 to 7, all different within a row; in each aligned block of 16 rows (0 to 15, 16 to 31, ..., all dimensions but the last counted through in order) at most 8 rows name the same one
- gate_weights: bfloat16 [4, 128, 2], P('section', 'expert'), may hold values from 0.099609375 to 1
- w_gate: bfloat16 [4, 6144, 4096], P('section', 'expert'), may hold values from -0.09375 to 0.09375
- w_up: bfloat16 [4, 6144, 4096], P('section', 'expert'), may hold values from -0.09375 to 0.09375
- w_down: bfloat16 [4, 6144, 4096], P('section', 'expert'), may hold values from -0.09375 to 0.09375
Outputs:
- passed_grad: bfloat16 [4, 128, 4096], P('section', 'expert')
- route_grad: float32 [4, 128, 2], P('section', 'expert')
The draws below stay inside these ranges and needn't reach their ends.
Inputs may be any that keep to these rules, and one draw needn't show every extreme that they name: `expert_ids`: the 2 experts of a token differ. Among the 16 tokens of one device no expert is named by more than 8 tokens, and in some device's rows some expert is named by exactly 8.
All inputs are finite; a program needn't handle non-finite values.
Results may differ from the reference program's by a relative error of at most 0.0057.
Values may be sent and summed in bfloat16 or wider, within the bound.
No kernel may reach another device: no remote copies, remote signals or barrier semaphores. Data moves between devices by JAX's collectives and lax.ppermute only.
A program may use at most 64 MiB of HBM per device.

```python
import math
import jax
import jax.numpy as jnp
import numpy as np
from jax import lax

D = 4096
HID = 768
EXPERTS = 8
TOPW = 2
TOK_DEV = 16
Q = 8
TOKENS = 128
LAYERS = 4
N_EXPERT = 8


def levels(own_key, extent, pieces, low, top_value):
    loudness, own = 1.0, jax.random.fold_in(own_key, 6)
    for dim, parts in pieces:
        steps = jnp.exp(jax.random.uniform(jax.random.fold_in(own, dim), (parts,), jnp.float32, low / len(pieces), top_value / len(pieces)))
        loudness = loudness * jnp.repeat(steps, extent[dim] // parts).reshape([-1 if axis == dim else 1 for axis in range(len(extent))])
    return loudness


def assign_block(key, own, number, rows, amount, top, most, skew):
    ranking = jax.random.permutation(key, amount)
    heavy_load, usual = shares(amount, rows * top, most, skew, True), shares(amount, rows * top, most, skew, False)
    places = jnp.arange(amount)

    def named(tallies, rotation):
        used = int((tallies > 0).sum())
        fixed = max(1, used // 4)
        passed = fixed + (places - fixed + rotation * (used - fixed)) % max(1, amount - fixed)
        return jnp.zeros((amount,), jnp.int32).at[ranking[jnp.where(places < fixed, places, passed)]].set(jnp.asarray(tallies, jnp.int32))

    tallies = jnp.where(number % 4 == 0, named(heavy_load, number // 4), named(usual, number - number // 4 - 1))
    mixed = jax.random.permutation(jax.random.fold_in(own, 3), amount)
    source_of, sink = mixed[0:amount // 2 * 2:2], mixed[1:amount // 2 * 2:2]
    slack = jnp.minimum(tallies[source_of] - 1, most - tallies[sink]) // 2
    slack = jnp.where((source_of == ranking[0]) | (sink == ranking[0]) | (tallies[sink] == 0), 0, jnp.maximum(slack, 0))
    passed = jax.random.randint(jax.random.fold_in(own, 4), (amount // 2,), 0, 1 << 20) % (slack + 1)
    tallies = tallies.at[source_of].add(-passed).at[sink].add(passed)
    members = jnp.searchsorted(jnp.cumsum(tallies), jnp.arange(rows * top), side="right").astype(jnp.int32)
    grid = members.reshape(top, rows).T
    grid = grid[jax.random.permutation(jax.random.fold_in(own, 1), rows)]
    rotation = jax.random.randint(jax.random.fold_in(own, 2), (rows, 1), 0, top)
    return jnp.take_along_axis(grid, (jnp.arange(top)[None, :] + rotation) % top, axis=1)


def shares(count, total, limit, skew, full):
    portions = [(1 << 20) // math.isqrt(standing ** skew) + 1 for standing in range(1, count + 1)]
    largest = limit if full else min(limit, max(-(-total // count), total * portions[0] // sum(portions)))
    least = 1 if total - largest >= count - 1 else 0
    given, rest = [largest] + [least] * (count - 1), total - largest - least * (count - 1)
    while rest > 0:
        free = [i for i in range(1, count) if given[i] < largest] or [i for i in range(1, count) if given[i] < limit]
        whole, left = sum([portions[i] for i in free]), rest
        for i in free:
            more = min(limit - given[i], max(1, left * portions[i] // whole), rest)
            given[i] = given[i] + more
            rest = rest - more
    return np.array(given)


def centred(key, shape, spread, most, cuts=(), held_as=jnp.bfloat16):
    result = spread * jax.random.normal(key, shape, jnp.float32)
    if cuts:
        result = result * levels(key, shape, cuts, -0.22, 0.18)
    return jnp.clip(result, -most, most).astype(held_as)


def setup_inputs(seed: int = 0) -> dict:
    streams_of = jax.random.split(jax.random.key(seed), 8)
    tokens_in = centred(streams_of[0], (LAYERS, TOKENS, D), 1.0, 6.0, ((0, 4), (1, 8)))
    out_grad = centred(streams_of[1], (LAYERS, TOKENS, D), 1.0, 6.0, ((0, 4), (1, 8)))
    expert_ids_keys = jax.random.split(jax.random.fold_in(streams_of[2], 1), LAYERS * TOKENS // TOK_DEV)
    expert_ids_turns = jax.random.permutation(jax.random.fold_in(streams_of[2], 3), LAYERS * TOKENS // TOK_DEV)
    expert_ids = jax.vmap(lambda own, number: assign_block(jax.random.fold_in(streams_of[2], 2), own, number, TOK_DEV, EXPERTS, TOPW, Q, 2))(expert_ids_keys, expert_ids_turns).reshape((LAYERS, TOKENS, TOPW))
    gate_weights = jnp.clip(0.099609375 + 0.9003906 * jax.random.uniform(streams_of[3], (LAYERS, TOKENS, TOPW), jnp.float32) ** levels(streams_of[3], (LAYERS, TOKENS, TOPW), ((0, 4), (1, 8)), -0.2, 0.2), 0.099609375, 1.0).astype(jnp.bfloat16)
    w_gate = centred(streams_of[4], (LAYERS, EXPERTS * HID, D), D ** -0.5, 0.09375, ((0, 4), (1, 8)))
    w_up = centred(streams_of[5], (LAYERS, EXPERTS * HID, D), D ** -0.5, 0.09375, ((0, 4), (1, 8)))
    w_down = centred(streams_of[6], (LAYERS, EXPERTS * HID, D), D ** -0.5, 0.09375, ((0, 4), (1, 8)))
    return {"tokens_in": tokens_in, "out_grad": out_grad, "expert_ids": expert_ids, "gate_weights": gate_weights, "w_gate": w_gate, "w_up": w_up, "w_down": w_down}


def layer_grads(inputs, upstream, routes, gate_vals, gate_mat, up_mat, down_mat):
    group_size = N_EXPERT // EXPERTS
    width = HID // group_size
    row_count = min(TOKENS, N_EXPERT * (TOK_DEV // 2))
    dims = (((1,), (1,)), ((), ()))

    def one_expert(carry, expert):
        total, grads_route = carry
        route_hit = routes == expert
        routed = jnp.sum(route_hit.astype(jnp.int32), axis=1)
        gate_col = jnp.sum(jnp.where(route_hit, gate_vals.astype(jnp.float32), jnp.float32(0.0)), axis=1)
        order = jnp.argsort(1 - routed, stable=True)[:row_count].astype(jnp.int32)
        rows_x = inputs[order]
        rows_dy = upstream[order]
        rows_g = gate_col[order]
        start = (expert * HID).astype(jnp.int32)
        w_g = lax.dynamic_slice_in_dim(gate_mat, start, HID, 0)
        w_u = lax.dynamic_slice_in_dim(up_mat, start, HID, 0)
        w_d = lax.dynamic_slice_in_dim(down_mat, start, HID, 0)
        gate_pre = lax.dot_general(rows_x, w_g, dims, preferred_element_type=jnp.float32)
        up_pre = lax.dot_general(rows_x, w_u, dims, preferred_element_type=jnp.float32)
        hidden_grad = lax.dot_general(rows_dy, w_d, dims, preferred_element_type=jnp.float32)
        sigmoid_val = jax.nn.sigmoid(gate_pre)
        activated = gate_pre * sigmoid_val
        slope = sigmoid_val * (1.0 + gate_pre * (1.0 - sigmoid_val))
        scaled = hidden_grad * rows_g[:, None]
        grad_gate = (scaled * up_pre * slope).astype(jnp.bfloat16)
        grad_up = (scaled * activated).astype(jnp.bfloat16)
        left_g = grad_gate.astype(jnp.float32).reshape(row_count, group_size, width)
        left_u = grad_up.astype(jnp.float32).reshape(row_count, group_size, width)
        right_g = w_g.astype(jnp.float32).reshape(group_size, width, D)
        right_u = w_u.astype(jnp.float32).reshape(group_size, width, D)
        partial_value = jnp.einsum("rgh,ghd->rgd", left_g, right_g) + jnp.einsum("rgh,ghd->rgd", left_u, right_u)
        partial_value = lax.optimization_barrier(partial_value.astype(jnp.bfloat16)).astype(jnp.float32)
        total = total.at[order].add(jnp.sum(partial_value, axis=1))
        scores = jnp.sum(activated * up_pre * hidden_grad, axis=1)
        score_full = jnp.zeros((TOKENS,), jnp.float32).at[order].add(scores)
        grads_route = grads_route + jnp.where(route_hit, score_full[:, None], jnp.float32(0.0))
        return (total, grads_route), None

    start_carry = (jnp.zeros((TOKENS, D), jnp.float32), jnp.zeros((TOKENS, TOPW), jnp.float32))
    (total, grads_route), _ = lax.scan(one_expert, start_carry, jnp.arange(EXPERTS, dtype=jnp.int32))
    return total.astype(jnp.bfloat16), grads_route


def reference(tokens_in, out_grad, expert_ids, gate_weights, w_gate, w_up, w_down):
    def per_layer(items):
        return layer_grads(*items)

    input_grad, grads_route = lax.map(per_layer, (tokens_in, out_grad, expert_ids, gate_weights, w_gate, w_up, w_down))
    return jnp.roll(input_grad, -1, axis=0), grads_route
```

```python
import functools

import jax
import jax.numpy as jnp
from jax import lax
from jax.experimental import pallas as pl
from jax.experimental.pallas import tpu as pltpu
from jax.sharding import PartitionSpec as P

EXPERTS = 8
LANES = 128
CHUNKS = 2
NT = (((1,), (1,)), ((), ()))
TN = (((0,), (0,)), ((), ()))
VMEM = pl.BlockSpec(memory_space=pltpu.VMEM)
HBM = pl.BlockSpec(memory_space=pltpu.HBM)


def shifted(array, axis, by):
    peers = lax.axis_size(axis)
    return lax.ppermute(array, axis, [(i, (i + by) % peers) for i in range(peers)])


def swapped(array, bits):
    peers = lax.axis_size("expert")
    return lax.ppermute(array, "expert", [(i, i ^ bits) for i in range(peers)])


def resident(array):
    return pltpu.with_memory_space_constraint(array, pltpu.VMEM)


def streamed(array):
    return pltpu.with_memory_space_constraint(array, pltpu.HBM)


def rows_of(near_ref, far_ref, columns):
    return jnp.concatenate([near_ref[:, columns], far_ref[:, columns]], axis=0)


def products(mat_ref, near_ref, far_ref, width):
    total = None
    step = 1024
    for start in range(0, width, step):
        columns = pl.ds(start, min(step, width - start))
        term = lax.dot_general(
            mat_ref[:, columns],
            rows_of(near_ref, far_ref, columns),
            NT,
            preferred_element_type=jnp.float32,
        )
        total = term if total is None else total + term
    return total


def load_kernel(gate_ref, upstream_ref, table_ref, gate_out, packed_out, sems):
    width = upstream_ref.shape[1]
    rows = pltpu.make_async_copy(upstream_ref, packed_out.at[:, pl.ds(0, width)], sems.at[0])
    gate = pltpu.make_async_copy(gate_ref, gate_out, sems.at[1])
    rows.start()
    gate.start()
    packed_out[:, width:] = table_ref[...]
    rows.wait()
    gate.wait()


def first_kernel(
    near_ref, far_ref, gate_ref, up_hbm, down_hbm, gate_pre_ref, up_pre_ref, up_out, down_out, sems
):
    width = gate_ref.shape[1]
    up_copy = pltpu.make_async_copy(up_hbm, up_out, sems.at[0])
    down_copy = pltpu.make_async_copy(down_hbm, down_out, sems.at[1])
    up_copy.start()
    down_copy.start()
    gate_pre_ref[...] = products(gate_ref, near_ref, far_ref, width)
    up_copy.wait()
    up_pre_ref[...] = products(up_out, near_ref, far_ref, width)
    down_copy.wait()


def second_kernel(
    group_size, near_ref, far_ref, down_ref, gate_pre_ref, up_pre_ref, grad_gate_ref, grad_up_ref, score_ref
):
    me = lax.axis_index("expert")
    width = down_ref.shape[1]
    hidden_grad = products(down_ref, near_ref, far_ref, width)
    table = rows_of(near_ref, far_ref, pl.ds(width, LANES))
    lane = lax.broadcasted_iota(jnp.int32, (8, LANES), 1)
    pick = jnp.where(lane == me // group_size, 1.0, 0.0).astype(jnp.bfloat16)
    weight = lax.dot_general(pick, table, NT, preferred_element_type=jnp.float32)[0:1, :]
    gate_pre = gate_pre_ref[...]
    up_pre = up_pre_ref[...]
    sigmoid_val = 1.0 / (1.0 + jnp.exp(-gate_pre))
    activated = gate_pre * sigmoid_val
    slope = sigmoid_val * (1.0 + gate_pre * (1.0 - sigmoid_val))
    scores = jnp.sum(activated * up_pre * hidden_grad, axis=0, keepdims=True)
    scaled = hidden_grad * weight
    grad_gate_ref[...] = (scaled * up_pre * slope).astype(jnp.bfloat16)
    grad_up_ref[...] = (scaled * activated).astype(jnp.bfloat16)
    scores = jnp.where(weight != 0.0, scores, 0.0)
    tokens = scores.shape[1]
    by_token = jnp.transpose(jnp.broadcast_to(scores, (LANES, tokens)))
    high = by_token.astype(jnp.bfloat16).astype(jnp.float32)
    low = by_token - high
    column = lax.broadcasted_iota(jnp.int32, (tokens, LANES), 1)
    half = LANES // 2
    score_ref[...] = jnp.where(
        column == me, high, jnp.where(column == me + half, low, 0.0)
    ).astype(jnp.bfloat16)


def third_kernel(first, span, grad_gate_ref, grad_up_ref, gate_ref, up_ref, score_ref, near_ref, far_ref):
    columns = pl.ds(first, span)
    partial_value = lax.dot_general(
        grad_gate_ref[...], gate_ref[:, columns], TN, preferred_element_type=jnp.float32
    )
    partial_value = partial_value + lax.dot_general(
        grad_up_ref[...], up_ref[:, columns], TN, preferred_element_type=jnp.float32
    )
    partial_value = partial_value.astype(jnp.bfloat16)
    half = near_ref.shape[0]
    near_ref[:, :span] = partial_value[:half]
    far_ref[:, :span] = partial_value[half:]
    if near_ref.shape[1] > span:
        near_ref[:, span:] = score_ref[:half, :]
        far_ref[:, span:] = score_ref[half:, :]


def params(megabytes):
    return pltpu.CompilerParams(vmem_limit_bytes=megabytes * 1024 * 1024)


def on_device(tokens_in, out_grad, expert_ids, gate_weights, w_gate, w_up, w_down):
    inputs = tokens_in[0]
    upstream = out_grad[0]
    routes = expert_ids[0]
    gate_vals = gate_weights[0]
    tok_rows, width = inputs.shape
    hidden = w_gate.shape[1]
    devices = lax.axis_size("expert")
    group_size = devices // EXPERTS
    half = tok_rows * devices // 2
    others = sorted(range(2, devices, 2), reverse=True)

    def gathered(block):
        parts = {0: block}
        for bits in others:
            parts[bits] = swapped(block, bits)
        near = jnp.concatenate([parts[bits] for bits in range(0, devices, 2)], axis=0)
        return near, swapped(near, 1)

    lanes = jnp.arange(LANES, dtype=jnp.int32)
    route_hit = routes[:, :, None] == lanes[None, None, :]
    table = jnp.sum(jnp.where(route_hit, gate_vals[:, :, None].astype(jnp.float32), 0.0), axis=1)
    near_x, far_x = gathered(inputs)
    matrix = jax.ShapeDtypeStruct((hidden, width), jnp.bfloat16)
    gate_mat, packed = pl.pallas_call(
        load_kernel,
        out_shape=(matrix, jax.ShapeDtypeStruct((tok_rows, width + LANES), jnp.bfloat16)),
        in_specs=[HBM, HBM, VMEM],
        out_specs=(VMEM, VMEM),
        scratch_shapes=[pltpu.SemaphoreType.DMA((2,))],
        compiler_params=params(8),
        cost_estimate=pl.CostEstimate(
            flops=0, bytes_accessed=4 * hidden * width, transcendentals=0
        ),
    )(streamed(w_gate[0]), streamed(upstream), table.astype(jnp.bfloat16))
    gate_mat = resident(gate_mat)
    near_dy, far_dy = gathered(packed)
    pre = jax.ShapeDtypeStruct((hidden, 2 * half), jnp.float32)
    gate_pre, up_pre, up_mat, down_mat = pl.pallas_call(
        first_kernel,
        out_shape=(pre, pre, matrix, matrix),
        in_specs=[VMEM, VMEM, VMEM, HBM, HBM],
        out_specs=(VMEM,) * 4,
        scratch_shapes=[pltpu.SemaphoreType.DMA((2,))],
        compiler_params=params(8),
        cost_estimate=pl.CostEstimate(
            flops=8 * half * hidden * width, bytes_accessed=8 * hidden * width, transcendentals=0
        ),
    )(resident(near_x), resident(far_x), gate_mat, streamed(w_up[0]), streamed(w_down[0]))
    up_mat = resident(up_mat)
    down_mat = resident(down_mat)
    grads = jax.ShapeDtypeStruct((hidden, 2 * half), jnp.bfloat16)
    grad_gate, grad_up, score_lanes = pl.pallas_call(
        functools.partial(second_kernel, group_size),
        out_shape=(grads, grads, jax.ShapeDtypeStruct((2 * half, LANES), jnp.bfloat16)),
        in_specs=[VMEM] * 5,
        out_specs=(VMEM, VMEM, VMEM),
        compiler_params=params(8),
    )(resident(near_dy), resident(far_dy), down_mat, resident(gate_pre), resident(up_pre))
    passed = []
    score_sum = None
    span = width // CHUNKS
    for chunk in range(CHUNKS):
        extra = LANES if chunk == 0 else 0
        out = jax.ShapeDtypeStruct((half, span + extra), jnp.bfloat16)
        near, far = pl.pallas_call(
            functools.partial(third_kernel, chunk * span, span),
            out_shape=(out, out),
            in_specs=[VMEM] * 5,
            out_specs=(VMEM, VMEM),
            compiler_params=params(8),
        )(resident(grad_gate), resident(grad_up), gate_mat, up_mat, resident(score_lanes))
        merged = near.astype(jnp.float32) + swapped(far, 1).astype(jnp.float32)
        merged = merged.astype(jnp.bfloat16)
        blocks = merged.reshape(devices // 2, tok_rows, span + extra)
        total = blocks[0].astype(jnp.float32)
        for bits in others:
            total = total + swapped(blocks[bits // 2], bits).astype(jnp.float32)
        if extra:
            score_sum = total[:, span:]
        passed.append(shifted(total[:, :span].astype(jnp.bfloat16), "section", -1))
    score_sum = score_sum[:, : LANES // 2] + score_sum[:, LANES // 2 :]
    owner = jnp.arange(LANES // 2, dtype=jnp.int32) // group_size
    mine = routes[:, :, None] == owner[None, None, :]
    grads_route = jnp.sum(jnp.where(mine, score_sum[:, None, :], 0.0), axis=2)
    return (jnp.concatenate(passed, axis=1)[None], grads_route[None])


def solution(mesh):
    return jax.shard_map(
        on_device,
        mesh=mesh,
        in_specs=(P("section", "expert", None),) * 7,
        out_specs=(P("section", "expert", None), P("section", "expert", None)),
        check_vma=False,
    )
```

```python
import functools

import jax
import jax.numpy as jnp
from jax import lax
from jax.experimental import pallas as pl
from jax.experimental.pallas import tpu as pltpu
from jax.sharding import PartitionSpec as P

EXPERTS = 8
LANES = 128
CHUNKS = 2
VMEM = pl.BlockSpec(memory_space=pltpu.VMEM)
HBM = pl.BlockSpec(memory_space=pltpu.HBM)


def shifted(array, axis, by):
    peers = lax.axis_size(axis)
    return lax.ppermute(array, axis, [(i, (i + by) % peers) for i in range(peers)])


def swapped(array, bits):
    peers = lax.axis_size("expert")
    return lax.ppermute(array, "expert", [(i, i ^ bits) for i in range(peers)])


def resident(array):
    return pltpu.with_memory_space_constraint(array, pltpu.VMEM)


def streamed(array):
    return pltpu.with_memory_space_constraint(array, pltpu.HBM)


def rows_of(near_ref, far_ref, columns):
    return jnp.concatenate([near_ref[:, columns], far_ref[:, columns]], axis=0)


def flip_kernel(after_ref, mat_ref, out_ref):
    step = 512
    width = mat_ref.shape[1]
    for start in range(0, width, step):
        columns = pl.ds(start, min(step, width - start))
        out_ref[columns, :] = mat_ref[:, columns].T


def products(near_ref, far_ref, flipped_ref):
    rows = rows_of(near_ref, far_ref, pl.ds(0, flipped_ref.shape[0]))
    return jnp.dot(rows, flipped_ref[...], preferred_element_type=jnp.float32)


def pack_kernel(upstream_hbm, routes_hbm, vals_hbm, a_hbm, b_hbm, c_hbm, packed_ref, routes_ref, vals_ref, sems):
    tok_rows, width = upstream_hbm.shape
    copies = [
        pltpu.make_async_copy(routes_hbm, routes_ref, sems.at[0]),
        pltpu.make_async_copy(vals_hbm, vals_ref, sems.at[1]),
        pltpu.make_async_copy(upstream_hbm, packed_ref.at[:, pl.ds(0, width)], sems.at[2]),
    ]
    for copy in copies:
        copy.start()
    for copy in copies[:2]:
        copy.wait()
    expert = lax.broadcasted_iota(jnp.int32, (LANES, tok_rows), 0)
    table = jnp.zeros((LANES, tok_rows), jnp.float32)
    for route in range(routes_ref.shape[0]):
        chosen = routes_ref[route : route + 1, :] == expert
        value = vals_ref[route : route + 1, :].astype(jnp.float32)
        table = table + jnp.where(chosen, value, 0.0)
    packed_ref[:, width:] = jnp.transpose(table).astype(jnp.bfloat16)
    copies[2].wait()


def first_kernel(near_ref, far_ref, gate_ref, up_ref, gate_pre_ref, up_pre_ref):
    gate_pre_ref[...] = products(near_ref, far_ref, gate_ref)
    up_pre_ref[...] = products(near_ref, far_ref, up_ref)


def second_kernel(
    group_size, near_ref, far_ref, down_ref, gate_pre_ref, up_pre_ref, grad_gate_ref, grad_up_ref, score_ref
):
    me = lax.axis_index("expert")
    hidden_grad = products(near_ref, far_ref, down_ref)
    table = rows_of(near_ref, far_ref, pl.ds(down_ref.shape[0], LANES)).astype(jnp.float32)
    column = lax.broadcasted_iota(jnp.int32, table.shape, 1)
    weight = jnp.sum(jnp.where(column == me // group_size, table, 0.0), axis=1, keepdims=True)
    gate_pre = gate_pre_ref[...]
    up_pre = up_pre_ref[...]
    sigmoid_val = 1.0 / (1.0 + jnp.exp(-gate_pre))
    activated = gate_pre * sigmoid_val
    slope = sigmoid_val * (1.0 + gate_pre * (1.0 - sigmoid_val))
    scores = jnp.sum(activated * up_pre * hidden_grad, axis=1, keepdims=True)
    scaled = hidden_grad * weight
    grad_gate_ref[...] = (scaled * up_pre * slope).astype(jnp.bfloat16)
    grad_up_ref[...] = (scaled * activated).astype(jnp.bfloat16)
    scores = jnp.where(weight != 0.0, scores, 0.0)
    high = scores.astype(jnp.bfloat16).astype(jnp.float32)
    low = scores - high
    half = LANES // 2
    score_ref[...] = jnp.where(
        column == me, high, jnp.where(column == me + half, low, 0.0)
    ).astype(jnp.bfloat16)


def third_kernel(first, span, grad_gate_ref, grad_up_ref, gate_ref, up_ref, score_ref, near_ref, far_ref):
    columns = pl.ds(first, span)
    partial_value = jnp.dot(
        grad_gate_ref[...], gate_ref[:, columns], preferred_element_type=jnp.float32
    )
    partial_value = partial_value + jnp.dot(
        grad_up_ref[...], up_ref[:, columns], preferred_element_type=jnp.float32
    )
    partial_value = partial_value.astype(jnp.bfloat16)
    half = near_ref.shape[0]
    near_ref[:, :span] = partial_value[:half]
    far_ref[:, :span] = partial_value[half:]
    if near_ref.shape[1] > span:
        near_ref[:, span:] = score_ref[:half, :]
        far_ref[:, span:] = score_ref[half:, :]


def params(megabytes):
    return pltpu.CompilerParams(vmem_limit_bytes=megabytes * 1024 * 1024)


def on_device(tokens_in, out_grad, expert_ids, gate_weights, w_gate, w_up, w_down):
    inputs = tokens_in[0]
    upstream = out_grad[0]
    routes = expert_ids[0]
    gate_vals = gate_weights[0]
    tok_rows, width = inputs.shape
    hidden = w_gate.shape[1]
    devices = lax.axis_size("expert")
    group_size = devices // EXPERTS
    half = tok_rows * devices // 2
    others = list(range(2, devices, 2))
    top = routes.shape[1]

    def sent(block):
        parts = {0: block}
        for bits in others:
            parts[bits] = swapped(block, bits)
        return [parts[bits] for bits in range(0, devices, 2)]

    parts_x = sent(inputs)
    packed = pl.pallas_call(
        pack_kernel,
        out_shape=jax.ShapeDtypeStruct((tok_rows, width + LANES), jnp.bfloat16),
        in_specs=[HBM] * 6,
        out_specs=VMEM,
        scratch_shapes=[
            pltpu.VMEM((top, tok_rows), jnp.int32),
            pltpu.VMEM((top, tok_rows), jnp.bfloat16),
            pltpu.SemaphoreType.DMA((3,)),
        ],
        compiler_params=params(4),
        cost_estimate=pl.CostEstimate(
            flops=0, bytes_accessed=12 * hidden * width, transcendentals=0
        ),
    )(streamed(upstream), streamed(routes.T), streamed(gate_vals.T), streamed(w_gate[0]), streamed(w_up[0]), streamed(w_down[0]))
    parts_dy = sent(packed)
    gate_mat = resident(w_gate[0])
    up_mat = resident(w_up[0])
    down_mat = resident(w_down[0])
    flip = pl.pallas_call(
        flip_kernel,
        out_shape=jax.ShapeDtypeStruct((width, hidden), jnp.bfloat16),
        in_specs=[VMEM, VMEM],
        out_specs=VMEM,
        compiler_params=params(4),
    )
    after = resident(parts_x[1])
    gate_flipped = resident(flip(after, gate_mat))
    up_flipped = resident(flip(after, up_mat))
    down_flipped = resident(flip(after, down_mat))
    parts_x, gate_flipped, up_flipped = lax.optimization_barrier((parts_x, gate_flipped, up_flipped))
    near_x = jnp.concatenate(parts_x, axis=0)
    far_x = swapped(near_x, 1)
    pre = jax.ShapeDtypeStruct((2 * half, hidden), jnp.float32)
    gate_pre, up_pre = pl.pallas_call(
        first_kernel,
        out_shape=(pre, pre),
        in_specs=[VMEM] * 4,
        out_specs=(VMEM,) * 2,
        compiler_params=params(8),
        cost_estimate=pl.CostEstimate(
            flops=8 * half * hidden * width, bytes_accessed=0, transcendentals=0
        ),
    )(resident(near_x), resident(far_x), gate_flipped, up_flipped)
    parts_dy, down_flipped = lax.optimization_barrier((parts_dy, down_flipped))
    near_dy = jnp.concatenate(parts_dy, axis=0)
    far_dy = swapped(near_dy, 1)
    grads = jax.ShapeDtypeStruct((2 * half, hidden), jnp.bfloat16)
    grad_gate, grad_up, score_lanes = pl.pallas_call(
        functools.partial(second_kernel, group_size),
        out_shape=(grads, grads, jax.ShapeDtypeStruct((2 * half, LANES), jnp.bfloat16)),
        in_specs=[VMEM] * 5,
        out_specs=(VMEM, VMEM, VMEM),
        compiler_params=params(8),
    )(resident(near_dy), resident(far_dy), down_flipped, resident(gate_pre), resident(up_pre))
    passed = []
    score_sum = None
    span = width // CHUNKS
    for chunk in range(CHUNKS):
        extra = LANES if chunk == 0 else 0
        out = jax.ShapeDtypeStruct((half, span + extra), jnp.bfloat16)
        near, far = pl.pallas_call(
            functools.partial(third_kernel, chunk * span, span),
            out_shape=(out, out),
            in_specs=[VMEM] * 5,
            out_specs=(VMEM, VMEM),
            compiler_params=params(8),
        )(resident(grad_gate), resident(grad_up), gate_mat, up_mat, resident(score_lanes))
        merged = near.astype(jnp.float32) + swapped(far, 1).astype(jnp.float32)
        merged = merged.astype(jnp.bfloat16)
        blocks = merged.reshape(devices // 2, tok_rows, span + extra)
        total = blocks[0].astype(jnp.float32)
        for bits in others:
            total = total + swapped(blocks[bits // 2], bits).astype(jnp.float32)
        if extra:
            score_sum = total[:, span:]
        passed.append(shifted(total[:, :span].astype(jnp.bfloat16), "section", -1))
    score_sum = score_sum[:, : LANES // 2] + score_sum[:, LANES // 2 :]
    owner = jnp.arange(LANES // 2, dtype=jnp.int32) // group_size
    mine = routes[:, :, None] == owner[None, None, :]
    grads_route = jnp.sum(jnp.where(mine, score_sum[:, None, :], 0.0), axis=2)
    return (jnp.concatenate(passed, axis=1)[None], grads_route[None])


def solution(mesh):
    return jax.shard_map(
        on_device,
        mesh=mesh,
        in_specs=(P("section", "expert", None),) * 7,
        out_specs=(P("section", "expert", None), P("section", "expert", None)),
        check_vma=False,
    )
```

```python
import functools

import jax
import jax.numpy as jnp
from jax import lax
from jax.experimental import pallas as pl
from jax.experimental.pallas import tpu as pltpu
from jax.sharding import PartitionSpec as P

EXPERTS = 8
LANES = 128
CHUNKS = 2
VMEM = pl.BlockSpec(memory_space=pltpu.VMEM)
HBM = pl.BlockSpec(memory_space=pltpu.HBM)


def shifted(array, axis, by):
    peers = lax.axis_size(axis)
    return lax.ppermute(array, axis, [(i, (i + by) % peers) for i in range(peers)])


def swapped(array, bits):
    peers = lax.axis_size("expert")
    return lax.ppermute(array, "expert", [(i, i ^ bits) for i in range(peers)])


def resident(array):
    return pltpu.with_memory_space_constraint(array, pltpu.VMEM)


def streamed(array):
    return pltpu.with_memory_space_constraint(array, pltpu.HBM)


def rows_of(near_ref, far_ref, columns):
    return jnp.concatenate([near_ref[:, columns], far_ref[:, columns]], axis=0)


def flip_kernel(after_ref, mat_ref, out_ref):
    step = 512
    width = mat_ref.shape[1]
    for start in range(0, width, step):
        columns = pl.ds(start, min(step, width - start))
        out_ref[columns, :] = mat_ref[:, columns].T


def products(near_ref, far_ref, flipped_ref):
    rows = rows_of(near_ref, far_ref, pl.ds(0, flipped_ref.shape[0]))
    return jnp.dot(rows, flipped_ref[...], preferred_element_type=jnp.float32)


def pack_kernel(upstream_hbm, routes_hbm, vals_ref, a_hbm, b_hbm, c_hbm, packed_ref, routes_ref, sems):
    tok_rows, width = upstream_hbm.shape
    copies = [
        pltpu.make_async_copy(routes_hbm, routes_ref, sems.at[0]),
        pltpu.make_async_copy(upstream_hbm, packed_ref.at[:, pl.ds(0, width)], sems.at[1]),
    ]
    for copy in copies:
        copy.start()
    copies[0].wait()
    expert = lax.broadcasted_iota(jnp.int32, (LANES, tok_rows), 0)
    table = jnp.zeros((LANES, tok_rows), jnp.float32)
    for route in range(routes_ref.shape[0]):
        chosen = routes_ref[route : route + 1, :] == expert
        value = vals_ref[route : route + 1, :].astype(jnp.float32)
        table = table + jnp.where(chosen, value, 0.0)
    packed_ref[:, width:] = jnp.transpose(table).astype(jnp.bfloat16)
    copies[1].wait()


def first_kernel(near_ref, far_ref, gate_ref, up_ref, gate_pre_ref, up_pre_ref):
    gate_pre_ref[...] = products(near_ref, far_ref, gate_ref)
    up_pre_ref[...] = products(near_ref, far_ref, up_ref)


def second_kernel(
    group_size, near_ref, far_ref, down_ref, gate_pre_ref, up_pre_ref, grad_gate_ref, grad_up_ref, score_ref
):
    me = lax.axis_index("expert")
    hidden_grad = products(near_ref, far_ref, down_ref)
    table = rows_of(near_ref, far_ref, pl.ds(down_ref.shape[0], LANES)).astype(jnp.float32)
    column = lax.broadcasted_iota(jnp.int32, table.shape, 1)
    weight = jnp.sum(jnp.where(column == me // group_size, table, 0.0), axis=1, keepdims=True)
    gate_pre = gate_pre_ref[...]
    up_pre = up_pre_ref[...]
    sigmoid_val = 1.0 / (1.0 + jnp.exp(-gate_pre))
    activated = gate_pre * sigmoid_val
    slope = sigmoid_val * (1.0 + gate_pre * (1.0 - sigmoid_val))
    scores = jnp.sum(activated * up_pre * hidden_grad, axis=1, keepdims=True)
    scaled = hidden_grad * weight
    grad_gate_ref[...] = (scaled * up_pre * slope).astype(jnp.bfloat16)
    grad_up_ref[...] = (scaled * activated).astype(jnp.bfloat16)
    scores = jnp.where(weight != 0.0, scores, 0.0)
    high = scores.astype(jnp.bfloat16).astype(jnp.float32)
    low = scores - high
    half = LANES // 2
    score_ref[...] = jnp.where(
        column == me, high, jnp.where(column == me + half, low, 0.0)
    ).astype(jnp.bfloat16)


def third_kernel(first, span, grad_gate_ref, grad_up_ref, gate_ref, up_ref, score_ref, near_ref, far_ref):
    columns = pl.ds(first, span)
    partial_value = jnp.dot(
        grad_gate_ref[...], gate_ref[:, columns], preferred_element_type=jnp.float32
    )
    partial_value = partial_value + jnp.dot(
        grad_up_ref[...], up_ref[:, columns], preferred_element_type=jnp.float32
    )
    partial_value = partial_value.astype(jnp.bfloat16)
    half = near_ref.shape[0]
    near_ref[:, :span] = partial_value[:half]
    far_ref[:, :span] = partial_value[half:]
    if near_ref.shape[1] > span:
        near_ref[:, span:] = score_ref[:half, :]
        far_ref[:, span:] = score_ref[half:, :]


def params(megabytes):
    return pltpu.CompilerParams(vmem_limit_bytes=megabytes * 1024 * 1024)


def on_device(tokens_in, out_grad, expert_ids, gate_weights, w_gate, w_up, w_down):
    inputs = tokens_in[0]
    upstream = out_grad[0]
    routes = expert_ids[0]
    gate_vals = gate_weights[0]
    tok_rows, width = inputs.shape
    hidden = w_gate.shape[1]
    devices = lax.axis_size("expert")
    group_size = devices // EXPERTS
    half = tok_rows * devices // 2
    others = list(range(2, devices, 2))
    top = routes.shape[1]

    def sent(block):
        parts = {0: block}
        for bits in others:
            parts[bits] = swapped(block, bits)
        return [parts[bits] for bits in range(0, devices, 2)]

    parts_x = sent(inputs)
    packed = pl.pallas_call(
        pack_kernel,
        out_shape=jax.ShapeDtypeStruct((tok_rows, width + LANES), jnp.bfloat16),
        in_specs=[HBM, HBM, VMEM, HBM, HBM, HBM],
        out_specs=VMEM,
        scratch_shapes=[
            pltpu.VMEM((top, tok_rows), jnp.int32),
            pltpu.SemaphoreType.DMA((2,)),
        ],
        compiler_params=params(4),
        cost_estimate=pl.CostEstimate(
            flops=0, bytes_accessed=12 * hidden * width, transcendentals=0
        ),
    )(streamed(upstream), streamed(routes.T), gate_vals.T, streamed(w_gate[0]), streamed(w_up[0]), streamed(w_down[0]))
    parts_dy = sent(packed)
    gate_mat = resident(w_gate[0])
    up_mat = resident(w_up[0])
    down_mat = resident(w_down[0])
    flip = pl.pallas_call(
        flip_kernel,
        out_shape=jax.ShapeDtypeStruct((width, hidden), jnp.bfloat16),
        in_specs=[VMEM, VMEM],
        out_specs=VMEM,
        compiler_params=params(4),
    )
    after = resident(parts_x[1])
    gate_flipped = resident(flip(after, gate_mat))
    up_flipped = resident(flip(after, up_mat))
    down_flipped = resident(flip(after, down_mat))
    parts_x, gate_flipped, up_flipped = lax.optimization_barrier((parts_x, gate_flipped, up_flipped))
    near_x = jnp.concatenate(parts_x, axis=0)
    far_x = swapped(near_x, 1)
    pre = jax.ShapeDtypeStruct((2 * half, hidden), jnp.float32)
    gate_pre, up_pre = pl.pallas_call(
        first_kernel,
        out_shape=(pre, pre),
        in_specs=[VMEM] * 4,
        out_specs=(VMEM,) * 2,
        compiler_params=params(8),
        cost_estimate=pl.CostEstimate(
            flops=8 * half * hidden * width, bytes_accessed=0, transcendentals=0
        ),
    )(resident(near_x), resident(far_x), gate_flipped, up_flipped)
    parts_dy, down_flipped = lax.optimization_barrier((parts_dy, down_flipped))
    near_dy = jnp.concatenate(parts_dy, axis=0)
    far_dy = swapped(near_dy, 1)
    grads = jax.ShapeDtypeStruct((2 * half, hidden), jnp.bfloat16)
    grad_gate, grad_up, score_lanes = pl.pallas_call(
        functools.partial(second_kernel, group_size),
        out_shape=(grads, grads, jax.ShapeDtypeStruct((2 * half, LANES), jnp.bfloat16)),
        in_specs=[VMEM] * 5,
        out_specs=(VMEM, VMEM, VMEM),
        compiler_params=params(8),
    )(resident(near_dy), resident(far_dy), down_flipped, resident(gate_pre), resident(up_pre))
    passed = []
    score_sum = None
    span = width // CHUNKS
    for chunk in range(CHUNKS):
        extra = LANES if chunk == 0 else 0
        out = jax.ShapeDtypeStruct((half, span + extra), jnp.bfloat16)
        near, far = pl.pallas_call(
            functools.partial(third_kernel, chunk * span, span),
            out_shape=(out, out),
            in_specs=[VMEM] * 5,
            out_specs=(VMEM, VMEM),
            compiler_params=params(8),
        )(resident(grad_gate), resident(grad_up), gate_mat, up_mat, resident(score_lanes))
        merged = near.astype(jnp.float32) + swapped(far, 1).astype(jnp.float32)
        merged = merged.astype(jnp.bfloat16)
        blocks = merged.reshape(devices // 2, tok_rows, span + extra)
        total = blocks[0].astype(jnp.float32)
        for bits in others:
            total = total + swapped(blocks[bits // 2], bits).astype(jnp.float32)
        if extra:
            score_sum = total[:, span:]
        passed.append(shifted(total[:, :span].astype(jnp.bfloat16), "section", -1))
    score_sum = score_sum[:, : LANES // 2] + score_sum[:, LANES // 2 :]
    owner = jnp.arange(LANES // 2, dtype=jnp.int32) // group_size
    mine = routes[:, :, None] == owner[None, None, :]
    grads_route = jnp.sum(jnp.where(mine, score_sum[:, None, :], 0.0), axis=2)
    return (jnp.concatenate(passed, axis=1)[None], grads_route[None])


def solution(mesh):
    return jax.shard_map(
        on_device,
        mesh=mesh,
        in_specs=(P("section", "expert", None),) * 7,
        out_specs=(P("section", "expert", None), P("section", "expert", None)),
        check_vma=False,
    )
```

```python
import functools

import jax
import jax.numpy as jnp
from jax import lax
from jax.experimental import pallas as pl
from jax.experimental.pallas import tpu as pltpu
from jax.sharding import PartitionSpec as P

EXPERTS = 8
LANES = 128
CHUNKS = 2
VMEM = pl.BlockSpec(memory_space=pltpu.VMEM)
HBM = pl.BlockSpec(memory_space=pltpu.HBM)


def shifted(array, axis, by):
    peers = lax.axis_size(axis)
    return lax.ppermute(array, axis, [(i, (i + by) % peers) for i in range(peers)])


def swapped(array, bits):
    peers = lax.axis_size("expert")
    return lax.ppermute(array, "expert", [(i, i ^ bits) for i in range(peers)])


def resident(array):
    return pltpu.with_memory_space_constraint(array, pltpu.VMEM)


def streamed(array):
    return pltpu.with_memory_space_constraint(array, pltpu.HBM)


def rows_of(near_ref, far_ref, columns):
    return jnp.concatenate([near_ref[:, columns], far_ref[:, columns]], axis=0)


def flip_kernel(after_ref, mat_ref, out_ref):
    step = 512
    width = mat_ref.shape[1]
    for start in range(0, width, step):
        columns = pl.ds(start, min(step, width - start))
        out_ref[columns, :] = mat_ref[:, columns].T


def products(near_ref, far_ref, flipped_ref):
    rows = rows_of(near_ref, far_ref, pl.ds(0, flipped_ref.shape[0]))
    return jnp.dot(rows, flipped_ref[...], preferred_element_type=jnp.float32)


def pack_kernel(upstream_hbm, routes_hbm, vals_ref, a_hbm, b_hbm, c_hbm, packed_ref, routes_ref, sems):
    tok_rows, width = upstream_hbm.shape
    copies = [
        pltpu.make_async_copy(routes_hbm, routes_ref, sems.at[0]),
        pltpu.make_async_copy(upstream_hbm, packed_ref.at[:, pl.ds(0, width)], sems.at[1]),
    ]
    for copy in copies:
        copy.start()
    copies[0].wait()
    expert = lax.broadcasted_iota(jnp.int32, (LANES, tok_rows), 0)
    table = jnp.zeros((LANES, tok_rows), jnp.float32)
    vals = vals_ref[...].astype(jnp.float32)
    for route in range(routes_ref.shape[0]):
        chosen = routes_ref[route : route + 1, :] == expert
        table = table + jnp.where(chosen, vals[route : route + 1, :], 0.0)
    packed_ref[:, width:] = jnp.transpose(table).astype(jnp.bfloat16)
    copies[1].wait()


def first_kernel(near_ref, far_ref, gate_ref, up_ref, gate_pre_ref, up_pre_ref):
    gate_pre_ref[...] = products(near_ref, far_ref, gate_ref)
    up_pre_ref[...] = products(near_ref, far_ref, up_ref)


def second_kernel(
    group_size, near_ref, far_ref, down_ref, gate_pre_ref, up_pre_ref, grad_gate_ref, grad_up_ref, score_ref
):
    me = lax.axis_index("expert")
    hidden_grad = products(near_ref, far_ref, down_ref)
    table = rows_of(near_ref, far_ref, pl.ds(down_ref.shape[0], LANES)).astype(jnp.float32)
    column = lax.broadcasted_iota(jnp.int32, table.shape, 1)
    weight = jnp.sum(jnp.where(column == me // group_size, table, 0.0), axis=1, keepdims=True)
    gate_pre = gate_pre_ref[...]
    up_pre = up_pre_ref[...]
    sigmoid_val = 1.0 / (1.0 + jnp.exp(-gate_pre))
    activated = gate_pre * sigmoid_val
    slope = sigmoid_val * (1.0 + gate_pre * (1.0 - sigmoid_val))
    scores = jnp.sum(activated * up_pre * hidden_grad, axis=1, keepdims=True)
    scaled = hidden_grad * weight
    grad_gate_ref[...] = (scaled * up_pre * slope).astype(jnp.bfloat16)
    grad_up_ref[...] = (scaled * activated).astype(jnp.bfloat16)
    scores = jnp.where(weight != 0.0, scores, 0.0)
    high = scores.astype(jnp.bfloat16).astype(jnp.float32)
    low = scores - high
    half = LANES // 2
    score_ref[...] = jnp.where(
        column == me, high, jnp.where(column == me + half, low, 0.0)
    ).astype(jnp.bfloat16)


def third_kernel(first, span, grad_gate_ref, grad_up_ref, gate_ref, up_ref, score_ref, near_ref, far_ref):
    columns = pl.ds(first, span)
    partial_value = jnp.dot(
        grad_gate_ref[...], gate_ref[:, columns], preferred_element_type=jnp.float32
    )
    partial_value = partial_value + jnp.dot(
        grad_up_ref[...], up_ref[:, columns], preferred_element_type=jnp.float32
    )
    partial_value = partial_value.astype(jnp.bfloat16)
    half = near_ref.shape[0]
    near_ref[:, :span] = partial_value[:half]
    far_ref[:, :span] = partial_value[half:]
    if near_ref.shape[1] > span:
        near_ref[:, span:] = score_ref[:half, :]
        far_ref[:, span:] = score_ref[half:, :]


def params(megabytes):
    return pltpu.CompilerParams(vmem_limit_bytes=megabytes * 1024 * 1024)


def on_device(tokens_in, out_grad, expert_ids, gate_weights, w_gate, w_up, w_down):
    inputs = tokens_in[0]
    upstream = out_grad[0]
    routes = expert_ids[0]
    gate_vals = gate_weights[0]
    tok_rows, width = inputs.shape
    hidden = w_gate.shape[1]
    devices = lax.axis_size("expert")
    group_size = devices // EXPERTS
    half = tok_rows * devices // 2
    others = list(range(2, devices, 2))
    top = routes.shape[1]

    def sent(block):
        parts = {0: block}
        for bits in others:
            parts[bits] = swapped(block, bits)
        return [parts[bits] for bits in range(0, devices, 2)]

    parts_x = sent(inputs)
    packed = pl.pallas_call(
        pack_kernel,
        out_shape=jax.ShapeDtypeStruct((tok_rows, width + LANES), jnp.bfloat16),
        in_specs=[HBM, HBM, VMEM, HBM, HBM, HBM],
        out_specs=VMEM,
        scratch_shapes=[
            pltpu.VMEM((top, tok_rows), jnp.int32),
            pltpu.SemaphoreType.DMA((2,)),
        ],
        compiler_params=params(4),
        cost_estimate=pl.CostEstimate(
            flops=0, bytes_accessed=12 * hidden * width, transcendentals=0
        ),
    )(streamed(upstream), streamed(routes.T), gate_vals.T, streamed(w_gate[0]), streamed(w_up[0]), streamed(w_down[0]))
    parts_dy = sent(packed)
    gate_mat = resident(w_gate[0])
    up_mat = resident(w_up[0])
    down_mat = resident(w_down[0])
    flip = pl.pallas_call(
        flip_kernel,
        out_shape=jax.ShapeDtypeStruct((width, hidden), jnp.bfloat16),
        in_specs=[VMEM, VMEM],
        out_specs=VMEM,
        compiler_params=params(4),
    )
    after = resident(parts_x[1])
    gate_flipped = resident(flip(after, gate_mat))
    up_flipped = resident(flip(after, up_mat))
    down_flipped = resident(flip(after, down_mat))
    parts_x, gate_flipped, up_flipped = lax.optimization_barrier((parts_x, gate_flipped, up_flipped))
    near_x = jnp.concatenate(parts_x, axis=0)
    far_x = swapped(near_x, 1)
    pre = jax.ShapeDtypeStruct((2 * half, hidden), jnp.float32)
    gate_pre, up_pre = pl.pallas_call(
        first_kernel,
        out_shape=(pre, pre),
        in_specs=[VMEM] * 4,
        out_specs=(VMEM,) * 2,
        compiler_params=params(8),
        cost_estimate=pl.CostEstimate(
            flops=8 * half * hidden * width, bytes_accessed=0, transcendentals=0
        ),
    )(resident(near_x), resident(far_x), gate_flipped, up_flipped)
    parts_dy, down_flipped = lax.optimization_barrier((parts_dy, down_flipped))
    near_dy = jnp.concatenate(parts_dy, axis=0)
    far_dy = swapped(near_dy, 1)
    grads = jax.ShapeDtypeStruct((2 * half, hidden), jnp.bfloat16)
    grad_gate, grad_up, score_lanes = pl.pallas_call(
        functools.partial(second_kernel, group_size),
        out_shape=(grads, grads, jax.ShapeDtypeStruct((2 * half, LANES), jnp.bfloat16)),
        in_specs=[VMEM] * 5,
        out_specs=(VMEM, VMEM, VMEM),
        compiler_params=params(8),
    )(resident(near_dy), resident(far_dy), down_flipped, resident(gate_pre), resident(up_pre))
    passed = []
    score_sum = None
    span = width // CHUNKS
    for chunk in range(CHUNKS):
        extra = LANES if chunk == 0 else 0
        out = jax.ShapeDtypeStruct((half, span + extra), jnp.bfloat16)
        near, far = pl.pallas_call(
            functools.partial(third_kernel, chunk * span, span),
            out_shape=(out, out),
            in_specs=[VMEM] * 5,
            out_specs=(VMEM, VMEM),
            compiler_params=params(8),
        )(resident(grad_gate), resident(grad_up), gate_mat, up_mat, resident(score_lanes))
        merged = near.astype(jnp.float32) + swapped(far, 1).astype(jnp.float32)
        merged = merged.astype(jnp.bfloat16)
        blocks = merged.reshape(devices // 2, tok_rows, span + extra)
        total = blocks[0].astype(jnp.float32)
        for bits in others:
            total = total + swapped(blocks[bits // 2], bits).astype(jnp.float32)
        if extra:
            score_sum = total[:, span:]
        passed.append(shifted(total[:, :span].astype(jnp.bfloat16), "section", -1))
    score_sum = score_sum[:, : LANES // 2] + score_sum[:, LANES // 2 :]
    owner = jnp.arange(LANES // 2, dtype=jnp.int32) // group_size
    mine = routes[:, :, None] == owner[None, None, :]
    grads_route = jnp.sum(jnp.where(mine, score_sum[:, None, :], 0.0), axis=2)
    return (jnp.concatenate(passed, axis=1)[None], grads_route[None])


def solution(mesh):
    return jax.shard_map(
        on_device,
        mesh=mesh,
        in_specs=(P("section", "expert", None),) * 7,
        out_specs=(P("section", "expert", None), P("section", "expert", None)),
        check_vma=False,
    )
```

```python
import functools

import jax
import jax.numpy as jnp
from jax import lax
from jax.experimental import pallas as pl
from jax.experimental.pallas import tpu as pltpu
from jax.sharding import PartitionSpec as P

EXPERTS = 8
LANES = 128
CHUNKS = 2
VMEM = pl.BlockSpec(memory_space=pltpu.VMEM)
HBM = pl.BlockSpec(memory_space=pltpu.HBM)


def shifted(array, axis, by):
    peers = lax.axis_size(axis)
    return lax.ppermute(array, axis, [(i, (i + by) % peers) for i in range(peers)])


def swapped(array, bits):
    peers = lax.axis_size("expert")
    return lax.ppermute(array, "expert", [(i, i ^ bits) for i in range(peers)])


def resident(array):
    return pltpu.with_memory_space_constraint(array, pltpu.VMEM)


def streamed(array):
    return pltpu.with_memory_space_constraint(array, pltpu.HBM)


def rows_of(near_ref, far_ref, columns):
    return jnp.concatenate([near_ref[:, columns], far_ref[:, columns]], axis=0)


def flip_pair_kernel(after_ref, gate_ref, up_ref, out_ref):
    step = 512
    hidden, width = gate_ref.shape
    for start in range(0, width, step):
        columns = pl.ds(start, min(step, width - start))
        out_ref[columns, :hidden] = gate_ref[:, columns].T
        out_ref[columns, hidden:] = up_ref[:, columns].T


def flip_kernel(after_ref, mat_ref, out_ref):
    step = 512
    width = mat_ref.shape[1]
    for start in range(0, width, step):
        columns = pl.ds(start, min(step, width - start))
        out_ref[columns, :] = mat_ref[:, columns].T


def products(near_ref, far_ref, flipped_ref):
    rows = rows_of(near_ref, far_ref, pl.ds(0, flipped_ref.shape[0]))
    return jnp.dot(rows, flipped_ref[...], preferred_element_type=jnp.float32)


def pack_kernel(upstream_hbm, routes_hbm, vals_ref, a_hbm, b_hbm, c_hbm, packed_ref, routes_ref, sems):
    tok_rows, width = upstream_hbm.shape
    copies = [
        pltpu.make_async_copy(routes_hbm, routes_ref, sems.at[0]),
        pltpu.make_async_copy(upstream_hbm, packed_ref.at[:, pl.ds(0, width)], sems.at[1]),
    ]
    for copy in copies:
        copy.start()
    copies[0].wait()
    expert = lax.broadcasted_iota(jnp.int32, (LANES, tok_rows), 0)
    table = jnp.zeros((LANES, tok_rows), jnp.float32)
    vals = vals_ref[...].astype(jnp.float32)
    for route in range(routes_ref.shape[0]):
        chosen = routes_ref[route : route + 1, :] == expert
        table = table + jnp.where(chosen, vals[route : route + 1, :], 0.0)
    packed_ref[:, width:] = jnp.transpose(table).astype(jnp.bfloat16)
    copies[1].wait()


def first_kernel(near_ref, far_ref, pair_ref, gate_pre_ref, up_pre_ref):
    both = products(near_ref, far_ref, pair_ref)
    hidden = gate_pre_ref.shape[1]
    gate_pre_ref[...] = both[:, :hidden]
    up_pre_ref[...] = both[:, hidden:]


def second_kernel(
    group_size, near_ref, far_ref, down_ref, gate_pre_ref, up_pre_ref, grad_gate_ref, grad_up_ref, score_ref
):
    me = lax.axis_index("expert")
    hidden_grad = products(near_ref, far_ref, down_ref)
    table = rows_of(near_ref, far_ref, pl.ds(down_ref.shape[0], LANES)).astype(jnp.float32)
    column = lax.broadcasted_iota(jnp.int32, table.shape, 1)
    weight = jnp.sum(jnp.where(column == me // group_size, table, 0.0), axis=1, keepdims=True)
    gate_pre = gate_pre_ref[...]
    up_pre = up_pre_ref[...]
    sigmoid_val = 1.0 / (1.0 + jnp.exp(-gate_pre))
    activated = gate_pre * sigmoid_val
    slope = sigmoid_val * (1.0 + gate_pre * (1.0 - sigmoid_val))
    scores = jnp.sum(activated * up_pre * hidden_grad, axis=1, keepdims=True)
    scaled = hidden_grad * weight
    grad_gate_ref[...] = (scaled * up_pre * slope).astype(jnp.bfloat16)
    grad_up_ref[...] = (scaled * activated).astype(jnp.bfloat16)
    scores = jnp.where(weight != 0.0, scores, 0.0)
    high = scores.astype(jnp.bfloat16).astype(jnp.float32)
    low = scores - high
    half = LANES // 2
    score_ref[...] = jnp.where(
        column == me, high, jnp.where(column == me + half, low, 0.0)
    ).astype(jnp.bfloat16)


def third_kernel(first, span, grad_gate_ref, grad_up_ref, gate_ref, up_ref, score_ref, near_ref, far_ref):
    columns = pl.ds(first, span)
    partial_value = jnp.dot(
        grad_gate_ref[...], gate_ref[:, columns], preferred_element_type=jnp.float32
    )
    partial_value = partial_value + jnp.dot(
        grad_up_ref[...], up_ref[:, columns], preferred_element_type=jnp.float32
    )
    partial_value = partial_value.astype(jnp.bfloat16)
    half = near_ref.shape[0]
    near_ref[:, :span] = partial_value[:half]
    far_ref[:, :span] = partial_value[half:]
    if near_ref.shape[1] > span:
        near_ref[:, span:] = score_ref[:half, :]
        far_ref[:, span:] = score_ref[half:, :]


def params(megabytes):
    return pltpu.CompilerParams(vmem_limit_bytes=megabytes * 1024 * 1024)


def on_device(tokens_in, out_grad, expert_ids, gate_weights, w_gate, w_up, w_down):
    inputs = tokens_in[0]
    upstream = out_grad[0]
    routes = expert_ids[0]
    gate_vals = gate_weights[0]
    tok_rows, width = inputs.shape
    hidden = w_gate.shape[1]
    devices = lax.axis_size("expert")
    group_size = devices // EXPERTS
    half = tok_rows * devices // 2
    others = list(range(2, devices, 2))
    top = routes.shape[1]

    def sent(block):
        parts = {0: block}
        for bits in others:
            parts[bits] = swapped(block, bits)
        return [parts[bits] for bits in range(0, devices, 2)]

    parts_x = sent(inputs)
    packed = pl.pallas_call(
        pack_kernel,
        out_shape=jax.ShapeDtypeStruct((tok_rows, width + LANES), jnp.bfloat16),
        in_specs=[HBM, HBM, VMEM, HBM, HBM, HBM],
        out_specs=VMEM,
        scratch_shapes=[
            pltpu.VMEM((top, tok_rows), jnp.int32),
            pltpu.SemaphoreType.DMA((2,)),
        ],
        compiler_params=params(4),
        cost_estimate=pl.CostEstimate(
            flops=0, bytes_accessed=12 * hidden * width, transcendentals=0
        ),
    )(streamed(upstream), streamed(routes.T), gate_vals.T, streamed(w_gate[0]), streamed(w_up[0]), streamed(w_down[0]))
    parts_dy = sent(packed)
    gate_mat = resident(w_gate[0])
    up_mat = resident(w_up[0])
    down_mat = resident(w_down[0])
    flip = pl.pallas_call(
        flip_kernel,
        out_shape=jax.ShapeDtypeStruct((width, hidden), jnp.bfloat16),
        in_specs=[VMEM, VMEM],
        out_specs=VMEM,
        compiler_params=params(4),
    )
    after = resident(parts_x[1])
    pair = resident(
        pl.pallas_call(
            flip_pair_kernel,
            out_shape=jax.ShapeDtypeStruct((width, 2 * hidden), jnp.bfloat16),
            in_specs=[VMEM] * 3,
            out_specs=VMEM,
            compiler_params=params(4),
        )(after, gate_mat, up_mat)
    )
    down_flipped = resident(flip(after, down_mat))
    parts_x, pair = lax.optimization_barrier((parts_x, pair))
    near_x = jnp.concatenate(parts_x, axis=0)
    far_x = swapped(near_x, 1)
    pre = jax.ShapeDtypeStruct((2 * half, hidden), jnp.float32)
    gate_pre, up_pre = pl.pallas_call(
        first_kernel,
        out_shape=(pre, pre),
        in_specs=[VMEM] * 3,
        out_specs=(VMEM,) * 2,
        compiler_params=params(8),
        cost_estimate=pl.CostEstimate(
            flops=8 * half * hidden * width, bytes_accessed=0, transcendentals=0
        ),
    )(resident(near_x), resident(far_x), pair)
    parts_dy, down_flipped = lax.optimization_barrier((parts_dy, down_flipped))
    near_dy = jnp.concatenate(parts_dy, axis=0)
    far_dy = swapped(near_dy, 1)
    grads = jax.ShapeDtypeStruct((2 * half, hidden), jnp.bfloat16)
    grad_gate, grad_up, score_lanes = pl.pallas_call(
        functools.partial(second_kernel, group_size),
        out_shape=(grads, grads, jax.ShapeDtypeStruct((2 * half, LANES), jnp.bfloat16)),
        in_specs=[VMEM] * 5,
        out_specs=(VMEM, VMEM, VMEM),
        compiler_params=params(8),
    )(resident(near_dy), resident(far_dy), down_flipped, resident(gate_pre), resident(up_pre))
    passed = []
    score_sum = None
    span = width // CHUNKS
    for chunk in range(CHUNKS):
        extra = LANES if chunk == 0 else 0
        out = jax.ShapeDtypeStruct((half, span + extra), jnp.bfloat16)
        near, far = pl.pallas_call(
            functools.partial(third_kernel, chunk * span, span),
            out_shape=(out, out),
            in_specs=[VMEM] * 5,
            out_specs=(VMEM, VMEM),
            compiler_params=params(8),
        )(resident(grad_gate), resident(grad_up), gate_mat, up_mat, resident(score_lanes))
        merged = near.astype(jnp.float32) + swapped(far, 1).astype(jnp.float32)
        merged = merged.astype(jnp.bfloat16)
        blocks = merged.reshape(devices // 2, tok_rows, span + extra)
        total = blocks[0].astype(jnp.float32)
        for bits in others:
            total = total + swapped(blocks[bits // 2], bits).astype(jnp.float32)
        if extra:
            score_sum = total[:, span:]
        passed.append(shifted(total[:, :span].astype(jnp.bfloat16), "section", -1))
    score_sum = score_sum[:, : LANES // 2] + score_sum[:, LANES // 2 :]
    owner = jnp.arange(LANES // 2, dtype=jnp.int32) // group_size
    mine = routes[:, :, None] == owner[None, None, :]
    grads_route = jnp.sum(jnp.where(mine, score_sum[:, None, :], 0.0), axis=2)
    return (jnp.concatenate(passed, axis=1)[None], grads_route[None])


def solution(mesh):
    return jax.shard_map(
        on_device,
        mesh=mesh,
        in_specs=(P("section", "expert", None),) * 7,
        out_specs=(P("section", "expert", None), P("section", "expert", None)),
        check_vma=False,
    )
```

```python
import functools

import jax
import jax.numpy as jnp
from jax import lax
from jax.experimental import pallas as pl
from jax.experimental.pallas import tpu as pltpu
from jax.sharding import PartitionSpec as P

EXPERTS = 8
LANES = 128
CHUNKS = 2
VMEM = pl.BlockSpec(memory_space=pltpu.VMEM)
HBM = pl.BlockSpec(memory_space=pltpu.HBM)


def shifted(array, axis, by):
    peers = lax.axis_size(axis)
    return lax.ppermute(array, axis, [(i, (i + by) % peers) for i in range(peers)])


def swapped(array, bits):
    peers = lax.axis_size("expert")
    return lax.ppermute(array, "expert", [(i, i ^ bits) for i in range(peers)])


def resident(array):
    return pltpu.with_memory_space_constraint(array, pltpu.VMEM)


def streamed(array):
    return pltpu.with_memory_space_constraint(array, pltpu.HBM)


def rows_of(near_ref, far_ref, columns):
    return jnp.concatenate([near_ref[:, columns], far_ref[:, columns]], axis=0)


def flip_pair_kernel(after_ref, gate_ref, up_ref, out_ref):
    step = 512
    hidden, width = gate_ref.shape
    for start in range(0, width, step):
        columns = pl.ds(start, min(step, width - start))
        out_ref[columns, :hidden] = gate_ref[:, columns].T
        out_ref[columns, hidden:] = up_ref[:, columns].T


def flip_kernel(after_ref, mat_ref, out_ref):
    step = 512
    width = mat_ref.shape[1]
    for start in range(0, width, step):
        columns = pl.ds(start, min(step, width - start))
        out_ref[columns, :] = mat_ref[:, columns].T


def products(near_ref, far_ref, flipped_ref):
    rows = rows_of(near_ref, far_ref, pl.ds(0, flipped_ref.shape[0]))
    return jnp.dot(rows, flipped_ref[...], preferred_element_type=jnp.float32)


def pack_kernel(upstream_hbm, routes_hbm, vals_ref, a_hbm, b_hbm, c_hbm, packed_ref, routes_ref, sems):
    tok_rows, width = upstream_hbm.shape
    copies = [
        pltpu.make_async_copy(routes_hbm, routes_ref, sems.at[0]),
        pltpu.make_async_copy(upstream_hbm, packed_ref.at[:, pl.ds(0, width)], sems.at[1]),
    ]
    for copy in copies:
        copy.start()
    copies[0].wait()
    expert = lax.broadcasted_iota(jnp.int32, (LANES, tok_rows), 0)
    table = jnp.zeros((LANES, tok_rows), jnp.float32)
    vals = vals_ref[...].astype(jnp.float32)
    for route in range(routes_ref.shape[0]):
        chosen = routes_ref[route : route + 1, :] == expert
        table = table + jnp.where(chosen, vals[route : route + 1, :], 0.0)
    packed_ref[:, width:] = jnp.transpose(table).astype(jnp.bfloat16)
    copies[1].wait()


def first_kernel(near_ref, far_ref, pair_ref, gate_pre_ref, up_pre_ref):
    both = products(near_ref, far_ref, pair_ref)
    hidden = gate_pre_ref.shape[1]
    gate_pre_ref[...] = both[:, :hidden]
    up_pre_ref[...] = both[:, hidden:]


def second_kernel(
    group_size, near_ref, far_ref, down_ref, gate_pre_ref, up_pre_ref, grad_gate_ref, grad_up_ref, score_ref
):
    me = lax.axis_index("expert")
    hidden_grad = products(near_ref, far_ref, down_ref)
    table = rows_of(near_ref, far_ref, pl.ds(down_ref.shape[0], LANES)).astype(jnp.float32)
    column = lax.broadcasted_iota(jnp.int32, table.shape, 1)
    weight = jnp.sum(jnp.where(column == me // group_size, table, 0.0), axis=1, keepdims=True)
    gate_pre = gate_pre_ref[...]
    up_pre = up_pre_ref[...]
    sigmoid_val = 1.0 / (1.0 + jnp.exp(-gate_pre))
    activated = gate_pre * sigmoid_val
    slope = sigmoid_val * (1.0 + gate_pre * (1.0 - sigmoid_val))
    scores = jnp.sum(activated * up_pre * hidden_grad, axis=1, keepdims=True)
    scaled = hidden_grad * weight
    grad_gate_ref[...] = (scaled * up_pre * slope).astype(jnp.bfloat16)
    grad_up_ref[...] = (scaled * activated).astype(jnp.bfloat16)
    scores = jnp.where(weight != 0.0, scores, 0.0)
    high = scores.astype(jnp.bfloat16).astype(jnp.float32)
    low = scores - high
    half = LANES // 2
    score_ref[...] = jnp.where(
        column == me, high, jnp.where(column == me + half, low, 0.0)
    ).astype(jnp.bfloat16)


def third_kernel(first, span, grad_gate_ref, grad_up_ref, gate_ref, up_ref, score_ref, near_ref, far_ref):
    columns = pl.ds(first, span)
    partial_value = jnp.dot(
        grad_gate_ref[...], gate_ref[:, columns], preferred_element_type=jnp.float32
    )
    partial_value = partial_value + jnp.dot(
        grad_up_ref[...], up_ref[:, columns], preferred_element_type=jnp.float32
    )
    partial_value = partial_value.astype(jnp.bfloat16)
    half = near_ref.shape[0]
    near_ref[:, :span] = partial_value[:half]
    far_ref[:, :span] = partial_value[half:]
    if near_ref.shape[1] > span:
        near_ref[:, span:] = score_ref[:half, :]
        far_ref[:, span:] = score_ref[half:, :]


def params(megabytes):
    return pltpu.CompilerParams(vmem_limit_bytes=megabytes * 1024 * 1024)


def on_device(tokens_in, out_grad, expert_ids, gate_weights, w_gate, w_up, w_down):
    inputs = tokens_in[0]
    upstream = out_grad[0]
    routes = expert_ids[0]
    gate_vals = gate_weights[0]
    tok_rows, width = inputs.shape
    hidden = w_gate.shape[1]
    devices = lax.axis_size("expert")
    group_size = devices // EXPERTS
    half = tok_rows * devices // 2
    others = list(range(2, devices, 2))
    top = routes.shape[1]

    def sent(block):
        parts = {0: block}
        for bits in others:
            parts[bits] = swapped(block, bits)
        return [parts[bits] for bits in range(0, devices, 2)]

    parts_x = sent(inputs)
    packed = pl.pallas_call(
        pack_kernel,
        out_shape=jax.ShapeDtypeStruct((tok_rows, width + LANES), jnp.bfloat16),
        in_specs=[HBM, HBM, VMEM, HBM, HBM, HBM],
        out_specs=VMEM,
        scratch_shapes=[
            pltpu.VMEM((top, tok_rows), jnp.int32),
            pltpu.SemaphoreType.DMA((2,)),
        ],
        compiler_params=params(4),
        cost_estimate=pl.CostEstimate(
            flops=0, bytes_accessed=12 * hidden * width, transcendentals=0
        ),
    )(streamed(upstream), streamed(routes.T), gate_vals.T, streamed(w_gate[0]), streamed(w_up[0]), streamed(w_down[0]))
    parts_dy = sent(packed)
    gate_mat = resident(w_gate[0])
    up_mat = resident(w_up[0])
    down_mat = resident(w_down[0])
    flip = pl.pallas_call(
        flip_kernel,
        out_shape=jax.ShapeDtypeStruct((width, hidden), jnp.bfloat16),
        in_specs=[VMEM, VMEM],
        out_specs=VMEM,
        compiler_params=params(4),
    )
    after = resident(parts_x[1])
    pair = resident(
        pl.pallas_call(
            flip_pair_kernel,
            out_shape=jax.ShapeDtypeStruct((width, 2 * hidden), jnp.bfloat16),
            in_specs=[VMEM] * 3,
            out_specs=VMEM,
            compiler_params=params(4),
        )(after, gate_mat, up_mat)
    )
    down_flipped = resident(flip(resident(parts_dy[1]), down_mat))
    parts_x, pair = lax.optimization_barrier((parts_x, pair))
    near_x = jnp.concatenate(parts_x, axis=0)
    far_x = swapped(near_x, 1)
    pre = jax.ShapeDtypeStruct((2 * half, hidden), jnp.float32)
    gate_pre, up_pre = pl.pallas_call(
        first_kernel,
        out_shape=(pre, pre),
        in_specs=[VMEM] * 3,
        out_specs=(VMEM,) * 2,
        compiler_params=params(8),
        cost_estimate=pl.CostEstimate(
            flops=8 * half * hidden * width, bytes_accessed=0, transcendentals=0
        ),
    )(resident(near_x), resident(far_x), pair)
    parts_dy, down_flipped = lax.optimization_barrier((parts_dy, down_flipped))
    near_dy = jnp.concatenate(parts_dy, axis=0)
    far_dy = swapped(near_dy, 1)
    grads = jax.ShapeDtypeStruct((2 * half, hidden), jnp.bfloat16)
    grad_gate, grad_up, score_lanes = pl.pallas_call(
        functools.partial(second_kernel, group_size),
        out_shape=(grads, grads, jax.ShapeDtypeStruct((2 * half, LANES), jnp.bfloat16)),
        in_specs=[VMEM] * 5,
        out_specs=(VMEM, VMEM, VMEM),
        compiler_params=params(8),
    )(resident(near_dy), resident(far_dy), down_flipped, resident(gate_pre), resident(up_pre))
    passed = []
    score_sum = None
    span = width // CHUNKS
    for chunk in range(CHUNKS):
        extra = LANES if chunk == 0 else 0
        out = jax.ShapeDtypeStruct((half, span + extra), jnp.bfloat16)
        near, far = pl.pallas_call(
            functools.partial(third_kernel, chunk * span, span),
            out_shape=(out, out),
            in_specs=[VMEM] * 5,
            out_specs=(VMEM, VMEM),
            compiler_params=params(8),
        )(resident(grad_gate), resident(grad_up), gate_mat, up_mat, resident(score_lanes))
        merged = near.astype(jnp.float32) + swapped(far, 1).astype(jnp.float32)
        merged = merged.astype(jnp.bfloat16)
        blocks = merged.reshape(devices // 2, tok_rows, span + extra)
        total = blocks[0].astype(jnp.float32)
        for bits in others:
            total = total + swapped(blocks[bits // 2], bits).astype(jnp.float32)
        if extra:
            score_sum = total[:, span:]
        passed.append(shifted(total[:, :span].astype(jnp.bfloat16), "section", -1))
    score_sum = score_sum[:, : LANES // 2] + score_sum[:, LANES // 2 :]
    owner = jnp.arange(LANES // 2, dtype=jnp.int32) // group_size
    mine = routes[:, :, None] == owner[None, None, :]
    grads_route = jnp.sum(jnp.where(mine, score_sum[:, None, :], 0.0), axis=2)
    return (jnp.concatenate(passed, axis=1)[None], grads_route[None])


def solution(mesh):
    return jax.shard_map(
        on_device,
        mesh=mesh,
        in_specs=(P("section", "expert", None),) * 7,
        out_specs=(P("section", "expert", None), P("section", "expert", None)),
        check_vma=False,
    )
```
